32 devices in a mesh: groups: 2 (over x), ctx: 16 (over z, y, core).
Axes of the slice: x: 2, y: 2, z: 4, core: 2. Of those that a mesh axis runs over, the one named last changes fastest.
Arguments:
- hidden: bfloat16 [8192, 14336], P(('groups', 'ctx')), parts along dimension 0, may hold values from -6 to 6
- out_grad: bfloat16 [8192, 4096], P(('groups', 'ctx')), parts along dimension 0, may hold values from -6 to 6
- in_proj: bfloat16 [14336, 64], replicated, may hold values from -0.046875 to 0.046875
- out_proj: bfloat16 [4096, 64], replicated, may hold values from -0.09375 to 0.09375
- doc_lengths: int32 [64], P('groups'), parts along dimension 0, may hold values from 1 to 1024, 4096 in all
- doc_slot: int32 [64], P('groups'), parts along dimension 0, may hold values from 0 to 31, each once
- queries: bfloat16 [256, 4096], P('ctx'), may hold values from -0.046875 to 0.046875
Outputs:
- scores: float32 [64, 256], P(('groups', 'ctx')), parts along dimension 0
The draws below stay inside these ranges and needn't reach their ends.
There are 2 independent parts, one for each index of `groups`. The reference program is written for one: setup_inputs(seed, part) draws one part's arguments, and reference() takes and returns one part's arrays. A program takes and returns all parts, laid end to end along the dimension named above; an argument that names none is the same for every part. Nothing has to cross between parts.
Inputs may be any that keep to these rules, and one draw needn't show every extreme that they name: `doc_lengths`: the lengths sum to 4096; the longest document has exactly 1024 tokens. `doc_slot`: each value names one document's output row, each once.
All inputs are finite; a program needn't handle non-finite values.
Results may differ from the reference program's by a relative error of at most 0.0003.
Values may be sent and summed in bfloat16 or wider, within the bound.
No kernel may reach another device: no remote copies, remote signals or barrier semaphores. Data moves between devices by JAX's collectives and lax.ppermute only.
A program may use at most 64 MiB of HBM per device.

```python
import math
import jax
import jax.numpy as jnp
import numpy as np
from jax import lax

D = 4096
FF = 14336
RANK = 64
TOK_DEV = 256
ROW = 4096
DOCS = 32
NQ = 256


def block_scale(stream_key, dims, cuts, least, high):
    def one(position, blocks):
        heights = jax.random.uniform(jax.random.fold_in(jax.random.fold_in(stream_key, 6), position), (blocks,), jnp.float32, least / len(cuts), high / len(cuts))
        return jnp.repeat(jnp.exp(heights), dims[position] // blocks).reshape((-1,) + (1,) * (len(dims) - position - 1))

    factor_of = one(*cuts[0])
    for cut in cuts[1:]:
        factor_of = factor_of * one(*cut)
    return factor_of


def split_up(amount, total, limit, slope):
    portions = [(1 << 20) // math.isqrt(standing ** slope) + 1 for standing in range(2, amount + 1)]
    spare, counts = total - limit - (amount - 1), [1] * (amount - 1)
    while spare > 0:
        movable = [i for i in range(amount - 1) if counts[i] < limit]
        mass, left = sum([portions[i] for i in movable]), spare
        for i in movable:
            extra = min(limit - counts[i], max(1, left * portions[i] // mass), spare)
            counts[i] = counts[i] + extra
            spare = spare - extra
    return np.array([limit] + counts)


def uneven(own_key, amount, total, most, slope):
    if amount == 2:
        one = jax.random.randint(own_key, (), max(1, total - most), min(most, total - 1) + 1)
        return jnp.stack([one, total - one])
    sizes = jnp.asarray(split_up(amount, total, most, slope), jnp.int32)
    twos = (amount - 1) // 2
    donor, taker = sizes[1:1 + 2 * twos:2], sizes[2:2 + 2 * twos:2]
    margin = jnp.minimum(donor - 1, most - taker)
    moved = jax.random.randint(jax.random.fold_in(own_key, 1), (twos,), 0, 1 << 20) % (margin + 1)
    sizes = sizes.at[1:1 + 2 * twos:2].set(donor - moved).at[2:2 + 2 * twos:2].set(taker + moved)
    return sizes[jax.random.permutation(jax.random.fold_in(own_key, 2), amount)]


def normal_values(key, extent, deviation, bound, cuts=(), kind=jnp.bfloat16):
    values = jax.random.normal(key, extent, jnp.float32) * deviation
    if len(cuts) > 0:
        values = block_scale(key, extent, cuts, -0.22, 0.18) * values
    return jnp.clip(values, min=-bound, max=bound).astype(kind)


def setup_inputs(seed: int = 0, part: int = 0) -> dict:
    arg_keys = jax.random.split(jax.random.key(seed), 8)
    part_splits = jax.random.split(jax.random.fold_in(arg_keys[7], part), 8)
    hidden = normal_values(part_splits[0], (ROW, FF), 1.0, 6.0, ((0, 16),))
    out_grad = normal_values(part_splits[1], (ROW, D), 1.0, 6.0, ((0, 16),))
    in_proj = normal_values(arg_keys[2], (FF, RANK), FF ** -0.5, 0.046875)
    out_proj = normal_values(arg_keys[3], (D, RANK), D ** -0.5, 0.09375)
    doc_lengths = uneven(part_splits[4], DOCS, ROW, 4 * TOK_DEV, 2).astype(jnp.int32)
    doc_slot = jax.random.permutation(part_splits[5], DOCS).astype(jnp.int32)
    queries = normal_values(arg_keys[6], (NQ, RANK * RANK), (4 * RANK * RANK) ** -0.5, 0.046875, ((0, 16),))
    return {"hidden": hidden, "out_grad": out_grad, "in_proj": in_proj, "out_proj": out_proj, "doc_lengths": doc_lengths, "doc_slot": doc_slot, "queries": queries}


def reference(hidden, out_grad, in_proj, out_proj, doc_lengths, doc_slot, queries):
    input_low = jnp.dot(hidden, in_proj, preferred_element_type=jnp.float32)
    grad_low = jnp.dot(out_grad, out_proj, preferred_element_type=jnp.float32)
    token_total = hidden.shape[0]
    doc_total = doc_slot.shape[0]
    doc_ends = jnp.cumsum(doc_lengths).astype(jnp.int32)
    positions = jnp.arange(token_total, dtype=jnp.int32)
    doc_index = jnp.sum((doc_ends[None, :] <= positions[:, None]).astype(jnp.int32), axis=1).astype(jnp.int32)
    slot_of_token = doc_slot[doc_index].astype(jnp.int32)
    outer_rows = (grad_low[:, :, None] * input_low[:, None, :]).reshape(token_total, -1)
    grads = jax.ops.segment_sum(outer_rows, slot_of_token, num_segments=doc_total)
    return jnp.dot(grads, queries.astype(jnp.float32).T, precision=lax.Precision.HIGHEST)
```

```python
import functools

import jax
import jax.numpy as jnp
from jax import lax
from jax.experimental import pallas as pl
from jax.experimental.pallas import tpu as pltpu
from jax.sharding import PartitionSpec as P

F32, BF16 = jnp.float32, jnp.bfloat16
LANES = 128
NT = (((1,), (1,)), ((), ()))


def split2(x):
    hi = x.astype(BF16)
    return hi, (x - hi.astype(F32)).astype(BF16)


def low_kernel(
    plan, hid, og, w_in, w_out, lengths, slots, keep, send,
    hid_v, og_v, w_in_v, w_out_v, pair_hi, pair_lo, sem,
):
    bits, hop_bits, k_bit, per_dev, docs, chunk = plan
    tokens = hid.shape[0]
    rank = w_in.shape[0]
    me = lax.axis_index("ctx")

    copies = []

    def fetch(src, dst, w_src, w_dst):
        steps = []
        for c in range(0, src.shape[1], chunk):
            cols = pl.ds(c, chunk)
            pair = []
            for s, d in ((src, dst), (w_src, w_dst)):
                copy = pltpu.make_async_copy(s.at[:, cols], d.at[:, cols], sem.at[len(copies)])
                copy.start()
                copies.append(copy)
                pair.append(copy)
            steps.append((cols, pair))
        return steps

    og_steps = fetch(og, og_v, w_out, w_out_v)
    hid_steps = fetch(hid, hid_v, w_in, w_in_v)

    lane = lax.broadcasted_iota(jnp.int32, (docs, docs), 1)
    sub = lax.broadcasted_iota(jnp.int32, (docs, docs), 0)
    length = jnp.broadcast_to(lengths[...], (docs, docs)).astype(F32)
    slot = jnp.broadcast_to(slots[...], (docs, docs)).astype(F32)
    ends = jnp.sum(jnp.where(lane <= sub, length, 0.0), axis=1, keepdims=True)
    starts = jnp.sum(jnp.where(lane < sub, length, 0.0), axis=1, keepdims=True)
    slot = jnp.sum(jnp.where(lane == sub, slot, 0.0), axis=1, keepdims=True).astype(jnp.int32)
    owner = slot // per_dev
    apart = owner ^ me
    row = jnp.zeros_like(slot)
    for b in hop_bits + (k_bit,):
        row = row * 2 + ((apart >> b) & 1)
    row = (row * per_dev + (slot - owner * per_dev)).astype(F32)
    token = (me * tokens + lax.broadcasted_iota(jnp.int32, (docs, tokens), 1)).astype(F32)
    inside = (token >= starts) & (token < ends)
    token_row = jnp.sum(jnp.where(inside, row, 0.0), axis=0, keepdims=True)

    def project(steps, src, w):
        total = jnp.zeros((rank, tokens), F32)
        for cols, pair in steps:
            for copy in pair:
                copy.wait()
            total += lax.dot_general(w[:, cols], src[:, cols], NT, preferred_element_type=F32)
        return total

    grad_low = project(og_steps, og_v, w_out_v)
    input_low = project(hid_steps, hid_v, w_in_v)

    half = rank // 4
    out_r = lax.broadcasted_iota(jnp.int32, (rank, rank), 0)
    in_r = lax.broadcasted_iota(jnp.int32, (rank, rank), 1)
    odd, p = out_r // (rank // 2), out_r % (rank // 2)
    mine = (me >> k_bit) & 1
    p = (p // half ^ mine) * half + p % half
    order = (in_r == 2 * p + odd).astype(BF16)
    g_hi, g_lo = split2(grad_low)
    g_hi = jnp.dot(order, g_hi, preferred_element_type=F32).astype(BF16)
    g_lo = jnp.dot(order, g_lo, preferred_element_type=F32).astype(BF16)
    pairs = rank // 2
    pair_hi[:, :tokens], pair_hi[:, tokens:] = g_hi[:pairs], g_hi[pairs:]
    pair_lo[:, :tokens], pair_lo[:, tokens:] = g_lo[:pairs], g_lo[pairs:]

    x_hi, x_lo = split2(input_low)
    zero = jnp.zeros_like(x_hi)

    def diagonal(x):
        return jnp.concatenate(
            [jnp.concatenate([x, zero], axis=1), jnp.concatenate([zero, x], axis=1)], axis=0
        )

    right_hi = diagonal(x_hi)
    right_both = jnp.concatenate([right_hi, diagonal(x_lo)], axis=0)

    in_block = 2 * per_dev
    blocks = docs // in_block
    for block in range(blocks):
        left_hi, left_lo = [], []
        for h in range(2):
            rows = pl.ds(h * half, half)
            for s in range(in_block):
                entry = block * in_block + (s + h * per_dev) % in_block
                hit = (token_row == float(entry)).astype(F32).astype(BF16)
                hit = jnp.concatenate([hit, hit], axis=1)
                left_hi.append(pair_hi[rows, :] * hit)
                left_lo.append(pair_lo[rows, :] * hit)
        left_hi, left_lo = jnp.concatenate(left_hi, axis=0), jnp.concatenate(left_lo, axis=0)
        both = lax.dot_general(left_hi, right_both, NT, preferred_element_type=F32)
        low = lax.dot_general(left_lo, right_hi, NT, preferred_element_type=F32)
        out = both[:, :LANES] + (both[:, LANES:] + low)
        size = out.shape[0]
        if block < blocks // 2:
            keep[pl.ds(block * size, size), :] = out
        else:
            send[pl.ds((block - blocks // 2) * size, size), :] = out


def score_kernel(plan, grads_a, grads_b, q_a, q_b, keep, send, left, columns, total):
    bits, q_bits, per_dev, per_q = plan
    me = lax.axis_index("ctx")
    rows = 2 * per_dev
    tiles = q_a.shape[1] // LANES
    total[...] = grads_a[...] + grads_b[...]
    pad = jnp.zeros((rows, LANES), BF16)
    for t in range(tiles):
        g = total[pl.ds(t, rows, stride=tiles), :]
        hi = g.astype(BF16)
        mid, low = split2(g - hi.astype(F32))
        left[:, pl.ds(t * LANES, LANES)] = jnp.concatenate([hi, mid, low, pad], axis=0)
    count = q_a.shape[0]
    for part, q in enumerate((q_a, q_b)):
        out = lax.dot_general(q[...], left[...], NT, preferred_element_type=F32)
        for i in range(count // per_q):
            index = part * (count // per_q) + i
            apart = 0
            for j, b in enumerate(reversed(q_bits)):
                apart = apart | (((index >> j) & 1) << b)
            at = pl.multiple_of((me ^ apart) * per_q, per_q)
            columns[pl.ds(at, per_q), :] = out[i * per_q:(i + 1) * per_q, :]
    out = columns[...].T
    out = out[:rows] + (out[rows:2 * rows] + out[2 * rows:3 * rows])
    keep[...] = out[:per_dev]
    send[...] = out[per_dev:]


def shards(n, hidden, out_grad, in_proj, out_proj, doc_lengths, doc_slot, queries):
    bits = n.bit_length() - 1
    tokens, ff = hidden.shape
    d, rank = out_proj.shape
    docs = doc_slot.shape[0]
    per_dev = docs // n
    per_q = queries.shape[0]
    k_bit = bits - 1
    hop_bits = tuple(range(bits - 1))
    me = lax.axis_index("ctx")

    def swap(x, b):
        return lax.ppermute(x, "ctx", [(i, i ^ (1 << b)) for i in range(n)])

    depth = queries.shape[1] // 2
    mine = (me >> k_bit) & 1
    q_keep = lax.dynamic_slice_in_dim(queries, mine * depth, depth, axis=1)
    q_send = lax.dynamic_slice_in_dim(queries, (1 - mine) * depth, depth, axis=1)
    q_bits = (k_bit,)
    q_parts = (q_keep, swap(q_send, k_bit))
    for b in hop_bits[1:] + hop_bits[:1]:
        q = jnp.concatenate(q_parts, axis=0)
        q_parts = (q, swap(q, b))
        q_bits = (b,) + q_bits

    chunk = 1024
    rows = docs * rank * rank // LANES
    any_spec = pl.BlockSpec(memory_space=pl.ANY)
    vmem = pl.BlockSpec(memory_space=pltpu.VMEM)
    half_shape = jax.ShapeDtypeStruct((rows // 2, LANES), F32)
    keep, send = pl.pallas_call(
        functools.partial(low_kernel, (bits, hop_bits, k_bit, per_dev, docs, chunk)),
        out_shape=(half_shape, half_shape),
        in_specs=[any_spec] * 4 + [vmem] * 2,
        out_specs=(vmem, vmem),
        scratch_shapes=[
            pltpu.VMEM((tokens, ff), BF16),
            pltpu.VMEM((tokens, d), BF16),
            pltpu.VMEM((rank, ff), BF16),
            pltpu.VMEM((rank, d), BF16),
            pltpu.VMEM((rank // 2, 2 * tokens), BF16),
            pltpu.VMEM((rank // 2, 2 * tokens), BF16),
            pltpu.SemaphoreType.DMA((2 * (ff + d) // chunk,)),
        ],
        compiler_params=pltpu.CompilerParams(vmem_limit_bytes=32 << 20),
        cost_estimate=pl.CostEstimate(
            flops=2 * tokens * rank * (ff + d),
            bytes_accessed=2 * (tokens + rank) * (ff + d),
            transcendentals=0,
        ),
        name="low",
    )(hidden, out_grad, in_proj.T, out_proj.T, doc_lengths.reshape(1, docs), doc_slot.reshape(1, docs))

    for b in hop_bits:
        got = swap(send, b)
        size = keep.shape[0] // 2
        total = keep + got
        keep, send = total[:size], total[size:]
    got = swap(send, k_bit)

    width = n * per_q
    small = jax.ShapeDtypeStruct((per_dev, width), F32)
    keep, send = pl.pallas_call(
        functools.partial(score_kernel, (bits, q_bits, per_dev, per_q)),
        out_shape=(small, small),
        in_specs=[vmem] * 4,
        out_specs=(vmem, vmem),
        scratch_shapes=[
            pltpu.VMEM((8 * per_dev, depth), BF16),
            pltpu.VMEM((width, 8 * per_dev), F32),
            pltpu.VMEM(keep.shape, F32),
        ],
        cost_estimate=pl.CostEstimate(
            flops=2 * width * depth * 8 * per_dev,
            bytes_accessed=2 * width * depth,
            transcendentals=0,
        ),
        compiler_params=pltpu.CompilerParams(vmem_limit_bytes=32 << 20),
        name="score",
    )(keep, got, *q_parts)
    return keep + swap(send, k_bit)


def solution(mesh):
    return jax.shard_map(
        functools.partial(shards, mesh.shape["ctx"]),
        mesh=mesh,
        in_specs=(
            P(("groups", "ctx"), None),
            P(("groups", "ctx"), None),
            P(),
            P(),
            P("groups"),
            P("groups"),
            P("ctx", None),
        ),
        out_specs=P(("groups", "ctx"), None),
        check_vma=False,
    )
```

```python
import functools

import jax
import jax.numpy as jnp
from jax import lax
from jax.experimental import pallas as pl
from jax.experimental.pallas import tpu as pltpu
from jax.sharding import PartitionSpec as P

F32, BF16 = jnp.float32, jnp.bfloat16
LANES = 128
NT = (((1,), (1,)), ((), ()))


def split2(x):
    hi = x.astype(BF16)
    return hi, (x - hi.astype(F32)).astype(BF16)


def low_kernel(
    plan, hid, og, w_in, w_out, documents, keep, send,
    hid_v, og_v, w_in_v, w_out_v, pair_hi, pair_lo, og_sem, hid_sem,
):
    bits, hop_bits, k_bit, per_dev, docs, og_chunk, hid_chunk = plan
    tokens = hid.shape[0]
    rank = w_in.shape[0]
    me = lax.axis_index("ctx")

    og_pairs, hid_pairs = ((og, og_v), (w_out, w_out_v)), ((hid, hid_v), (w_in, w_in_v))

    def fetches(i, pairs, sems, chunk):
        cols = pl.ds(pl.multiple_of(i * chunk, chunk), chunk)
        return cols, [
            pltpu.make_async_copy(src.at[:, cols], dst.at[:, cols], sems.at[j, i])
            for j, (src, dst) in enumerate(pairs)
        ]

    for pairs, sems, chunk in ((og_pairs, og_sem, og_chunk), (hid_pairs, hid_sem, hid_chunk)):
        for i in range(pairs[0][0].shape[1] // chunk):
            for copy in fetches(i, pairs, sems, chunk)[1]:
                copy.start()

    lane = lax.broadcasted_iota(jnp.int32, (docs, docs), 1)
    sub = lax.broadcasted_iota(jnp.int32, (docs, docs), 0)
    length = jnp.broadcast_to(documents[0:1, :], (docs, docs)).astype(F32)
    slot = jnp.broadcast_to(documents[1:2, :], (docs, docs)).astype(F32)
    ends = jnp.sum(jnp.where(lane <= sub, length, 0.0), axis=1, keepdims=True)
    starts = jnp.sum(jnp.where(lane < sub, length, 0.0), axis=1, keepdims=True)
    slot = jnp.sum(jnp.where(lane == sub, slot, 0.0), axis=1, keepdims=True).astype(jnp.int32)
    owner = slot // per_dev
    apart = owner ^ me
    row = jnp.zeros_like(slot)
    for b in hop_bits + (k_bit,):
        row = row * 2 + ((apart >> b) & 1)
    row = (row * per_dev + (slot - owner * per_dev)).astype(F32)
    token = (me * tokens + lax.broadcasted_iota(jnp.int32, (docs, tokens), 1)).astype(F32)
    inside = (token >= starts) & (token < ends)
    token_row = jnp.sum(jnp.where(inside, row, 0.0), axis=0, keepdims=True)

    def project(pairs, sems, chunk):
        (src, values), (_, weights) = pairs

        def step(i, total):
            cols, copies = fetches(i, pairs, sems, chunk)
            for copy in copies:
                copy.wait()
            return total + lax.dot_general(
                weights[:, cols], values[:, cols], NT, preferred_element_type=F32
            )

        return lax.fori_loop(0, src.shape[1] // chunk, step, jnp.zeros((rank, tokens), F32))

    grad_low = project(og_pairs, og_sem, og_chunk)
    input_low = project(hid_pairs, hid_sem, hid_chunk)

    half = rank // 4
    out_r = lax.broadcasted_iota(jnp.int32, (rank, rank), 0)
    in_r = lax.broadcasted_iota(jnp.int32, (rank, rank), 1)
    odd, p = out_r // (rank // 2), out_r % (rank // 2)
    mine = (me >> k_bit) & 1
    p = (p // half ^ mine) * half + p % half
    order = (in_r == 2 * p + odd).astype(BF16)
    g_hi, g_lo = split2(grad_low)
    g_hi = jnp.dot(order, g_hi, preferred_element_type=F32).astype(BF16)
    g_lo = jnp.dot(order, g_lo, preferred_element_type=F32).astype(BF16)
    pairs = rank // 2
    pair_hi[:, :tokens], pair_hi[:, tokens:] = g_hi[:pairs], g_hi[pairs:]
    pair_lo[:, :tokens], pair_lo[:, tokens:] = g_lo[:pairs], g_lo[pairs:]

    x_hi, x_lo = split2(input_low)
    zero = jnp.zeros_like(x_hi)

    def diagonal(x):
        return jnp.concatenate(
            [jnp.concatenate([x, zero], axis=1), jnp.concatenate([zero, x], axis=1)], axis=0
        )

    right_hi = diagonal(x_hi)
    right_both = jnp.concatenate([right_hi, diagonal(x_lo)], axis=0)

    in_block = 2 * per_dev
    blocks = docs // in_block
    for block in range(blocks):
        left_hi, left_lo = [], []
        for h in range(2):
            rows = pl.ds(h * half, half)
            for s in range(in_block):
                entry = block * in_block + (s + h * per_dev) % in_block
                hit = (token_row == float(entry)).astype(F32).astype(BF16)
                hit = jnp.concatenate([hit, hit], axis=1)
                left_hi.append(pair_hi[rows, :] * hit)
                left_lo.append(pair_lo[rows, :] * hit)
        left_hi, left_lo = jnp.concatenate(left_hi, axis=0), jnp.concatenate(left_lo, axis=0)
        both = lax.dot_general(left_hi, right_both, NT, preferred_element_type=F32)
        low = lax.dot_general(left_lo, right_hi, NT, preferred_element_type=F32)
        out = both[:, :LANES] + (both[:, LANES:] + low)
        size = out.shape[0]
        if block < blocks // 2:
            keep[pl.ds(block * size, size), :] = out
        else:
            send[pl.ds((block - blocks // 2) * size, size), :] = out


def near_kernel(per_dev, grads_a, grads_b, q, left, out, total):
    rows = 2 * per_dev
    tiles = q.shape[1] // LANES
    total[...] = grads_a[...] + grads_b[...]
    pad = jnp.zeros((rows, LANES), BF16)
    for t in range(tiles):
        g = total[pl.ds(t, rows, stride=tiles), :]
        hi = g.astype(BF16)
        mid, low = split2(g - hi.astype(F32))
        left[:, pl.ds(t * LANES, LANES)] = jnp.concatenate([hi, mid, low, pad], axis=0)
    out[...] = lax.dot_general(q[...], left[...], NT, preferred_element_type=F32)


def score_kernel(q_bits, per_dev, per_q, left, out_a, q_b, keep, send, columns):
    me = lax.axis_index("ctx")
    rows = 2 * per_dev
    count = q_b.shape[0]
    out_b = lax.dot_general(q_b[...], left[...], NT, preferred_element_type=F32)
    for part, out in enumerate((out_a[...], out_b)):
        for i in range(count // per_q):
            index = part * (count // per_q) + i
            apart = 0
            for j, b in enumerate(reversed(q_bits)):
                apart = apart | (((index >> j) & 1) << b)
            at = pl.multiple_of((me ^ apart) * per_q, per_q)
            columns[pl.ds(at, per_q), :] = out[i * per_q:(i + 1) * per_q, :]
    out = columns[...].T
    out = out[:rows] + (out[rows:2 * rows] + out[2 * rows:3 * rows])
    keep[...] = out[:per_dev]
    send[...] = out[per_dev:]


def shards(n, hidden, out_grad, in_proj, out_proj, doc_lengths, doc_slot, queries):
    bits = n.bit_length() - 1
    tokens, ff = hidden.shape
    d, rank = out_proj.shape
    docs = doc_slot.shape[0]
    per_dev = docs // n
    per_q = queries.shape[0]
    k_bit = bits - 1
    hop_bits = tuple(range(bits - 1))
    me = lax.axis_index("ctx")

    def swap(x, b):
        return lax.ppermute(x, "ctx", [(i, i ^ (1 << b)) for i in range(n)])

    depth = queries.shape[1] // 2
    mine = (me >> k_bit) & 1
    q_keep = lax.dynamic_slice_in_dim(queries, mine * depth, depth, axis=1)
    q_send = lax.dynamic_slice_in_dim(queries, (1 - mine) * depth, depth, axis=1)
    q_bits = (k_bit,)
    q_parts = (q_keep, swap(q_send, k_bit))
    for b in hop_bits[::-1]:
        q = jnp.concatenate(q_parts, axis=0)
        q_parts = (q, swap(q, b))
        q_bits = (b,) + q_bits

    og_chunk, hid_chunk = 2048, 3584
    rows = docs * rank * rank // LANES
    any_spec = pl.BlockSpec(memory_space=pl.ANY)
    vmem = pl.BlockSpec(memory_space=pltpu.VMEM)
    half_shape = jax.ShapeDtypeStruct((rows // 2, LANES), F32)
    keep, send = pl.pallas_call(
        functools.partial(low_kernel, (bits, hop_bits, k_bit, per_dev, docs, og_chunk, hid_chunk)),
        out_shape=(half_shape, half_shape),
        in_specs=[any_spec] * 4 + [vmem],
        out_specs=(vmem, vmem),
        scratch_shapes=[
            pltpu.VMEM((tokens, ff), BF16),
            pltpu.VMEM((tokens, d), BF16),
            pltpu.VMEM((rank, ff), BF16),
            pltpu.VMEM((rank, d), BF16),
            pltpu.VMEM((rank // 2, 2 * tokens), BF16),
            pltpu.VMEM((rank // 2, 2 * tokens), BF16),
            pltpu.SemaphoreType.DMA((2, d // og_chunk)),
            pltpu.SemaphoreType.DMA((2, ff // hid_chunk)),
        ],
        compiler_params=pltpu.CompilerParams(vmem_limit_bytes=53 << 20),
        cost_estimate=pl.CostEstimate(
            flops=2 * tokens * rank * (ff + d),
            bytes_accessed=2 * (tokens + rank) * (ff + d),
            transcendentals=0,
        ),
        name="low",
    )(hidden, out_grad, in_proj.T, out_proj.T, jnp.stack([doc_lengths, doc_slot]))

    for b in hop_bits:
        got = swap(send, b)
        size = keep.shape[0] // 2
        total = keep + got
        keep, send = total[:size], total[size:]
    got = swap(send, k_bit)

    width = n * per_q
    terms = 8 * per_dev
    left, out = pl.pallas_call(
        functools.partial(near_kernel, per_dev),
        out_shape=(
            jax.ShapeDtypeStruct((terms, depth), BF16),
            jax.ShapeDtypeStruct((width // 2, terms), F32),
        ),
        in_specs=[vmem] * 3,
        out_specs=(vmem, vmem),
        scratch_shapes=[pltpu.VMEM(keep.shape, F32)],
        compiler_params=pltpu.CompilerParams(vmem_limit_bytes=32 << 20),
        cost_estimate=pl.CostEstimate(flops=1 << 34, bytes_accessed=1 << 26, transcendentals=0),
        name="near_scores",
    )(keep, got, q_parts[0])
    small = jax.ShapeDtypeStruct((per_dev, width), F32)
    keep, send = pl.pallas_call(
        functools.partial(score_kernel, q_bits, per_dev, per_q),
        out_shape=(small, small),
        in_specs=[vmem] * 3,
        out_specs=(vmem, vmem),
        scratch_shapes=[pltpu.VMEM((width, terms), F32)],
        compiler_params=pltpu.CompilerParams(vmem_limit_bytes=32 << 20),
        name="scores",
    )(left, out, q_parts[1])
    return keep + swap(send, k_bit)


def solution(mesh):
    return jax.shard_map(
        functools.partial(shards, mesh.shape["ctx"]),
        mesh=mesh,
        in_specs=(
            P(("groups", "ctx"), None),
            P(("groups", "ctx"), None),
            P(),
            P(),
            P("groups"),
            P("groups"),
            P("ctx", None),
        ),
        out_specs=P(("groups", "ctx"), None),
        check_vma=False,
    )
```

```python
import functools

import jax
import jax.numpy as jnp
from jax import lax
from jax.experimental import pallas as pl
from jax.experimental.pallas import tpu as pltpu
from jax.sharding import PartitionSpec as P

F32, BF16 = jnp.float32, jnp.bfloat16
LANES = 128
NT = (((1,), (1,)), ((), ()))


def split2(x):
    hi = x.astype(BF16)
    return hi, (x - hi.astype(F32)).astype(BF16)


def low_kernel(
    plan, hid, og, w_in, w_out, documents, keep, send,
    hid_v, og_v, w_in_v, w_out_v, pair_hi, pair_lo, left, og_sem, hid_sem,
):
    bits, hop_bits, k_bit, per_dev, docs, og_chunk, hid_chunk = plan
    tokens = hid.shape[0]
    rank = w_in.shape[0]
    me = lax.axis_index("ctx")

    og_pairs, hid_pairs = ((og, og_v), (w_out, w_out_v)), ((hid, hid_v), (w_in, w_in_v))

    def fetches(i, pairs, sems, chunk):
        cols = pl.ds(pl.multiple_of(i * chunk, chunk), chunk)
        return cols, [
            pltpu.make_async_copy(src.at[:, cols], dst.at[:, cols], sems.at[j, i])
            for j, (src, dst) in enumerate(pairs)
        ]

    for i in range(hid.shape[1] // hid_chunk):
        for pairs, sems, chunk in ((og_pairs, og_sem, og_chunk), (hid_pairs, hid_sem, hid_chunk)):
            for copy in fetches(i, pairs, sems, chunk)[1]:
                copy.start()

    lane = lax.broadcasted_iota(jnp.int32, (docs, docs), 1)
    sub = lax.broadcasted_iota(jnp.int32, (docs, docs), 0)
    length = jnp.broadcast_to(documents[0:1, :], (docs, docs)).astype(F32)
    slot = jnp.broadcast_to(documents[1:2, :], (docs, docs)).astype(F32)
    ends = jnp.sum(jnp.where(lane <= sub, length, 0.0), axis=1, keepdims=True)
    starts = jnp.sum(jnp.where(lane < sub, length, 0.0), axis=1, keepdims=True)
    slot = jnp.sum(jnp.where(lane == sub, slot, 0.0), axis=1, keepdims=True).astype(jnp.int32)
    owner = slot // per_dev
    apart = owner ^ me
    row = jnp.zeros_like(slot)
    for b in hop_bits + (k_bit,):
        row = row * 2 + ((apart >> b) & 1)
    row = (row * per_dev + (slot - owner * per_dev)).astype(F32)
    token = (me * tokens + lax.broadcasted_iota(jnp.int32, (docs, tokens), 1)).astype(F32)
    inside = (token >= starts) & (token < ends)
    token_row = jnp.sum(jnp.where(inside, row, 0.0), axis=0, keepdims=True)

    def step(i, totals):
        fetched = [
            (pairs, *fetches(i, pairs, sems, chunk))
            for pairs, sems, chunk in ((og_pairs, og_sem, og_chunk), (hid_pairs, hid_sem, hid_chunk))
        ]
        for _, _, copies in fetched:
            for copy in copies:
                copy.wait()
        return tuple(
            total + lax.dot_general(x[:, cols], w[:, cols], NT, preferred_element_type=F32)
            for total, (((_, x), (_, w)), cols, _) in zip(totals, fetched)
        )

    zeros = jnp.zeros((tokens, rank), F32)
    grad_low, input_low = lax.fori_loop(0, hid.shape[1] // hid_chunk, step, (zeros, zeros))
    grad_low, input_low = grad_low.T, input_low.T

    half = rank // 4
    out_r = lax.broadcasted_iota(jnp.int32, (rank, rank), 0)
    in_r = lax.broadcasted_iota(jnp.int32, (rank, rank), 1)
    odd, p = out_r // (rank // 2), out_r % (rank // 2)
    mine = (me >> k_bit) & 1
    p = (p // half ^ mine) * half + p % half
    order = (in_r == 2 * p + odd).astype(BF16)
    g_hi, g_lo = split2(grad_low)
    g_hi = jnp.dot(order, g_hi, preferred_element_type=F32).astype(BF16)
    g_lo = jnp.dot(order, g_lo, preferred_element_type=F32).astype(BF16)
    pairs = rank // 2
    pair_hi[:, :tokens], pair_hi[:, tokens:] = g_hi[:pairs], g_hi[pairs:]
    pair_lo[:, :tokens], pair_lo[:, tokens:] = g_lo[:pairs], g_lo[pairs:]

    x_hi, x_lo = split2(input_low)
    zero = jnp.zeros_like(x_hi)

    def diagonal(x):
        return jnp.concatenate(
            [jnp.concatenate([x, zero], axis=1), jnp.concatenate([zero, x], axis=1)], axis=0
        )

    right = jnp.concatenate([diagonal(x_hi), diagonal(x_lo)], axis=0)
    right = jnp.concatenate([right, right], axis=1)

    in_block = 2 * per_dev
    blocks = docs // in_block
    row = 0
    for block in range(blocks):
        for h in range(2):
            rows = pl.ds(h * half, half)
            for s in range(in_block):
                entry = block * in_block + (s + h * per_dev) % in_block
                hit = (token_row == float(entry)).astype(F32).astype(BF16)
                hit = jnp.concatenate([hit, hit], axis=1)
                left[row:row + half, :2 * tokens] = pair_hi[rows, :] * hit
                left[row:row + half, 2 * tokens:] = pair_lo[rows, :] * hit
                row += half
    size = keep.shape[0]
    for part, out_ref in enumerate((send, keep)):
        rows = left[(1 - part) * size:(2 - part) * size, :]
        both = lax.dot_general(rows, right, NT, preferred_element_type=F32)
        out_ref[...] = both[:, :LANES] + both[:, LANES:]


def near_kernel(per_dev, grads_a, grads_b, q, left, out, total):
    rows = 2 * per_dev
    tiles = q.shape[1] // LANES
    total[...] = grads_a[...] + grads_b[...]
    pad = jnp.zeros((rows, LANES), BF16)
    for t in range(tiles):
        g = total[pl.ds(t, rows, stride=tiles), :]
        hi = g.astype(BF16)
        mid, low = split2(g - hi.astype(F32))
        left[:, pl.ds(t * LANES, LANES)] = jnp.concatenate([hi, mid, low, pad], axis=0)
    out[...] = lax.dot_general(q[...], left[...], NT, preferred_element_type=F32)


def score_kernel(q_bits, per_dev, per_q, left, out_a, q_b, keep, send, columns):
    me = lax.axis_index("ctx")
    rows = 2 * per_dev
    count = q_b.shape[0]
    out_b = lax.dot_general(q_b[...], left[...], NT, preferred_element_type=F32)
    for part, out in enumerate((out_a[...], out_b)):
        for i in range(count // per_q):
            index = part * (count // per_q) + i
            apart = 0
            for j, b in enumerate(reversed(q_bits)):
                apart = apart | (((index >> j) & 1) << b)
            at = pl.multiple_of((me ^ apart) * per_q, per_q)
            columns[pl.ds(at, per_q), :] = out[i * per_q:(i + 1) * per_q, :]
    out = columns[...].T
    out = out[:rows] + (out[rows:2 * rows] + out[2 * rows:3 * rows])
    keep[...] = out[:per_dev]
    send[...] = out[per_dev:]


def shards(n, hidden, out_grad, in_proj, out_proj, doc_lengths, doc_slot, queries):
    bits = n.bit_length() - 1
    tokens, ff = hidden.shape
    d, rank = out_proj.shape
    docs = doc_slot.shape[0]
    per_dev = docs // n
    per_q = queries.shape[0]
    k_bit = bits - 1
    hop_bits = tuple(range(bits - 1))
    me = lax.axis_index("ctx")

    def swap(x, b):
        return lax.ppermute(x, "ctx", [(i, i ^ (1 << b)) for i in range(n)])

    depth = queries.shape[1] // 2
    mine = (me >> k_bit) & 1
    q_keep = lax.dynamic_slice_in_dim(queries, mine * depth, depth, axis=1)
    q_send = lax.dynamic_slice_in_dim(queries, (1 - mine) * depth, depth, axis=1)
    q_bits = (k_bit,)
    q_parts = (q_keep, swap(q_send, k_bit))
    og_chunk, hid_chunk = 1024, 3584
    rows = docs * rank * rank // LANES
    any_spec = pl.BlockSpec(memory_space=pl.ANY)
    vmem = pl.BlockSpec(memory_space=pltpu.VMEM)
    half_shape = jax.ShapeDtypeStruct((rows // 2, LANES), F32)
    keep, send = pl.pallas_call(
        functools.partial(low_kernel, (bits, hop_bits, k_bit, per_dev, docs, og_chunk, hid_chunk)),
        out_shape=(half_shape, half_shape),
        in_specs=[any_spec] * 4 + [vmem],
        out_specs=(vmem, vmem),
        scratch_shapes=[
            pltpu.VMEM((tokens, ff), BF16),
            pltpu.VMEM((tokens, d), BF16),
            pltpu.VMEM((rank, ff), BF16),
            pltpu.VMEM((rank, d), BF16),
            pltpu.VMEM((rank // 2, 2 * tokens), BF16),
            pltpu.VMEM((rank // 2, 2 * tokens), BF16),
            pltpu.VMEM((rows, 4 * tokens), BF16),
            pltpu.SemaphoreType.DMA((2, d // og_chunk)),
            pltpu.SemaphoreType.DMA((2, ff // hid_chunk)),
        ],
        compiler_params=pltpu.CompilerParams(vmem_limit_bytes=53 << 20),
        cost_estimate=pl.CostEstimate(
            flops=2 * tokens * rank * (ff + d),
            bytes_accessed=2 * (tokens + rank) * (ff + d),
            transcendentals=0,
        ),
        name="low",
    )(hidden, out_grad, in_proj.T, out_proj.T, jnp.stack([doc_lengths, doc_slot]))

    sums = []
    for b in hop_bits:
        got = swap(send, b)
        size = keep.shape[0] // 2
        total = keep + got
        sums.append(total)
        keep, send = total[:size], total[size:]
    for i, b in enumerate(hop_bits[::-1]):
        q = jnp.concatenate(q_parts, axis=0)
        if i == 1:
            q, _ = lax.optimization_barrier((q, sums[0]))
        q_parts = (q, swap(q, b))
        q_bits = (b,) + q_bits
    got = swap(send, k_bit)

    width = n * per_q
    terms = 8 * per_dev
    left, out = pl.pallas_call(
        functools.partial(near_kernel, per_dev),
        out_shape=(
            jax.ShapeDtypeStruct((terms, depth), BF16),
            jax.ShapeDtypeStruct((width // 2, terms), F32),
        ),
        in_specs=[vmem] * 3,
        out_specs=(vmem, vmem),
        scratch_shapes=[pltpu.VMEM(keep.shape, F32)],
        compiler_params=pltpu.CompilerParams(vmem_limit_bytes=32 << 20),
        cost_estimate=pl.CostEstimate(flops=7000000000, bytes_accessed=1 << 20, transcendentals=0),
        name="near_scores",
    )(keep, got, q_parts[0])
    small = jax.ShapeDtypeStruct((per_dev, width), F32)
    keep, send = pl.pallas_call(
        functools.partial(score_kernel, q_bits, per_dev, per_q),
        out_shape=(small, small),
        in_specs=[vmem] * 3,
        out_specs=(vmem, vmem),
        scratch_shapes=[pltpu.VMEM((width, terms), F32)],
        compiler_params=pltpu.CompilerParams(vmem_limit_bytes=32 << 20),
        name="scores",
    )(left, out, q_parts[1])
    return keep + swap(send, k_bit)


def solution(mesh):
    return jax.shard_map(
        functools.partial(shards, mesh.shape["ctx"]),
        mesh=mesh,
        in_specs=(
            P(("groups", "ctx"), None),
            P(("groups", "ctx"), None),
            P(),
            P(),
            P("groups"),
            P("groups"),
            P("ctx", None),
        ),
        out_specs=P(("groups", "ctx"), None),
        check_vma=False,
    )
```

```python
import functools

import jax
import jax.numpy as jnp
from jax import lax
from jax.experimental import pallas as pl
from jax.experimental.pallas import tpu as pltpu
from jax.sharding import PartitionSpec as P

F32, BF16 = jnp.float32, jnp.bfloat16
LANES = 128
NT = (((1,), (1,)), ((), ()))


def split2(x):
    hi = x.astype(BF16)
    return hi, (x - hi.astype(F32)).astype(BF16)


def low_kernel(
    plan, hid, og, w_in, w_out, documents, keep, send,
    hid_v, og_v, w_in_v, w_out_v, pair_hi, pair_lo, left, og_sem, hid_sem,
):
    bits, hop_bits, k_bit, per_dev, docs, og_chunk, hid_chunk = plan
    tokens = hid.shape[0]
    rank = w_in.shape[0]
    me = lax.axis_index("ctx")

    og_pairs, hid_pairs = ((og, og_v), (w_out, w_out_v)), ((hid, hid_v), (w_in, w_in_v))

    def fetches(i, pairs, sems, chunk):
        cols = pl.ds(pl.multiple_of(i * chunk, chunk), chunk)
        return cols, [
            pltpu.make_async_copy(src.at[:, cols], dst.at[:, cols], sems.at[j, i])
            for j, (src, dst) in enumerate(pairs)
        ]

    for i in range(hid.shape[1] // hid_chunk):
        for pairs, sems, chunk in ((og_pairs, og_sem, og_chunk), (hid_pairs, hid_sem, hid_chunk)):
            for copy in fetches(i, pairs, sems, chunk)[1]:
                copy.start()

    lane = lax.broadcasted_iota(jnp.int32, (docs, docs), 1)
    sub = lax.broadcasted_iota(jnp.int32, (docs, docs), 0)
    length = jnp.broadcast_to(documents[0:1, :], (docs, docs)).astype(F32)
    slot = jnp.broadcast_to(documents[1:2, :], (docs, docs)).astype(F32)
    ends = jnp.sum(jnp.where(lane <= sub, length, 0.0), axis=1, keepdims=True)
    starts = jnp.sum(jnp.where(lane < sub, length, 0.0), axis=1, keepdims=True)
    slot = jnp.sum(jnp.where(lane == sub, slot, 0.0), axis=1, keepdims=True).astype(jnp.int32)
    owner = slot // per_dev
    apart = owner ^ me
    row = jnp.zeros_like(slot)
    for b in hop_bits + (k_bit,):
        row = row * 2 + ((apart >> b) & 1)
    row = (row * per_dev + (slot - owner * per_dev)).astype(F32)
    token = (me * tokens + lax.broadcasted_iota(jnp.int32, (docs, tokens), 1)).astype(F32)
    inside = (token >= starts) & (token < ends)
    token_row = jnp.sum(jnp.where(inside, row, 0.0), axis=0, keepdims=True)

    def step(i, totals):
        fetched = [
            (pairs, *fetches(i, pairs, sems, chunk))
            for pairs, sems, chunk in ((og_pairs, og_sem, og_chunk), (hid_pairs, hid_sem, hid_chunk))
        ]
        for _, _, copies in fetched:
            for copy in copies:
                copy.wait()
        (_, og_cols, _), (_, hid_cols, _) = fetched
        start, size = hid_cols.start, hid_chunk // 2
        parts = (
            (og_v, w_out_v, og_cols),
            (hid_v, w_in_v, pl.ds(start, size)),
            (hid_v, w_in_v, pl.ds(pl.multiple_of(start + size, size), size)),
        )
        return tuple(
            total + lax.dot_general(x[:, cols], w[:, cols], NT, preferred_element_type=F32)
            for total, (x, w, cols) in zip(totals, parts)
        )

    zeros = jnp.zeros((tokens, rank), F32)
    grad_low, first, second = lax.fori_loop(0, hid.shape[1] // hid_chunk, step, (zeros,) * 3)
    input_low = first + second
    grad_low, input_low = grad_low.T, input_low.T

    half = rank // 4
    out_r = lax.broadcasted_iota(jnp.int32, (rank, rank), 0)
    in_r = lax.broadcasted_iota(jnp.int32, (rank, rank), 1)
    odd, p = out_r // (rank // 2), out_r % (rank // 2)
    mine = (me >> k_bit) & 1
    p = (p // half ^ mine) * half + p % half
    order = (in_r == 2 * p + odd).astype(BF16)
    g_hi, g_lo = split2(grad_low)
    g_hi = jnp.dot(order, g_hi, preferred_element_type=F32).astype(BF16)
    g_lo = jnp.dot(order, g_lo, preferred_element_type=F32).astype(BF16)
    pairs = rank // 2
    pair_hi[:, :tokens], pair_hi[:, tokens:] = g_hi[:pairs], g_hi[pairs:]
    pair_lo[:, :tokens], pair_lo[:, tokens:] = g_lo[:pairs], g_lo[pairs:]

    x_hi, x_lo = split2(input_low)
    zero = jnp.zeros_like(x_hi)

    def diagonal(x):
        return jnp.concatenate(
            [jnp.concatenate([x, zero], axis=1), jnp.concatenate([zero, x], axis=1)], axis=0
        )

    right = jnp.concatenate([diagonal(x_hi), diagonal(x_lo)], axis=0)
    right = jnp.concatenate([right, right], axis=1)

    in_block = 2 * per_dev
    blocks = docs // in_block
    row = 0
    for block in range(blocks):
        for h in range(2):
            rows = pl.ds(h * half, half)
            for s in range(in_block):
                entry = block * in_block + (s + h * per_dev) % in_block
                hit = (token_row == float(entry)).astype(F32).astype(BF16)
                hit = jnp.concatenate([hit, hit], axis=1)
                left[row:row + half, :2 * tokens] = pair_hi[rows, :] * hit
                left[row:row + half, 2 * tokens:] = pair_lo[rows, :] * hit
                row += half
    size = keep.shape[0]
    for part, out_ref in enumerate((send, keep)):
        rows = left[(1 - part) * size:(2 - part) * size, :]
        both = lax.dot_general(rows, right, NT, preferred_element_type=F32)
        out_ref[...] = both[:, :LANES] + both[:, LANES:]


def near_kernel(per_dev, grads_a, grads_b, q, left, out, total):
    rows = 2 * per_dev
    tiles = q.shape[1] // LANES
    total[...] = grads_a[...] + grads_b[...]
    pad = jnp.zeros((rows, LANES), BF16)
    for t in range(tiles):
        g = total[pl.ds(t, rows, stride=tiles), :]
        hi = g.astype(BF16)
        mid, low = split2(g - hi.astype(F32))
        left[:, pl.ds(t * LANES, LANES)] = jnp.concatenate([hi, mid, low, pad], axis=0)
    out[...] = lax.dot_general(q[...], left[...], NT, preferred_element_type=F32)


def score_kernel(q_bits, per_dev, per_q, left, out_a, q_b, keep, send, columns):
    me = lax.axis_index("ctx")
    rows = 2 * per_dev
    count = q_b.shape[0]
    out_b = lax.dot_general(q_b[...], left[...], NT, preferred_element_type=F32)
    for part, out in enumerate((out_a[...], out_b)):
        for i in range(count // per_q):
            index = part * (count // per_q) + i
            apart = 0
            for j, b in enumerate(reversed(q_bits)):
                apart = apart | (((index >> j) & 1) << b)
            at = pl.multiple_of((me ^ apart) * per_q, per_q)
            columns[pl.ds(at, per_q), :] = out[i * per_q:(i + 1) * per_q, :]
    out = columns[...].T
    out = out[:rows] + (out[rows:2 * rows] + out[2 * rows:3 * rows])
    keep[...] = out[:per_dev]
    send[...] = out[per_dev:]


def shards(n, hidden, out_grad, in_proj, out_proj, doc_lengths, doc_slot, queries):
    bits = n.bit_length() - 1
    tokens, ff = hidden.shape
    d, rank = out_proj.shape
    docs = doc_slot.shape[0]
    per_dev = docs // n
    per_q = queries.shape[0]
    k_bit, top = 2, bits - 1
    hop_bits = tuple(b for b in range(bits) if b != k_bit)
    me = lax.axis_index("ctx")

    def swap(x, b):
        return lax.ppermute(x, "ctx", [(i, i ^ (1 << b)) for i in range(n)])

    depth = queries.shape[1] // 2
    mine = (me >> k_bit) & 1
    got_queries = swap(queries, top)
    og_chunk, hid_chunk = 1024, 3584
    rows = docs * rank * rank // LANES
    any_spec = pl.BlockSpec(memory_space=pl.ANY)
    vmem = pl.BlockSpec(memory_space=pltpu.VMEM)
    half_shape = jax.ShapeDtypeStruct((rows // 2, LANES), F32)
    keep, send = pl.pallas_call(
        functools.partial(low_kernel, (bits, hop_bits, k_bit, per_dev, docs, og_chunk, hid_chunk)),
        out_shape=(half_shape, half_shape),
        in_specs=[any_spec] * 4 + [vmem],
        out_specs=(vmem, vmem),
        scratch_shapes=[
            pltpu.VMEM((tokens, ff), BF16),
            pltpu.VMEM((tokens, d), BF16),
            pltpu.VMEM((rank, ff), BF16),
            pltpu.VMEM((rank, d), BF16),
            pltpu.VMEM((rank // 2, 2 * tokens), BF16),
            pltpu.VMEM((rank // 2, 2 * tokens), BF16),
            pltpu.VMEM((rows, 4 * tokens), BF16),
            pltpu.SemaphoreType.DMA((2, d // og_chunk)),
            pltpu.SemaphoreType.DMA((2, ff // hid_chunk)),
        ],
        compiler_params=pltpu.CompilerParams(vmem_limit_bytes=53 << 20),
        cost_estimate=pl.CostEstimate(
            flops=2 * tokens * rank * (ff + d),
            bytes_accessed=2 * (tokens + rank) * (ff + d),
            transcendentals=0,
        ),
        name="low",
    )(hidden, out_grad, in_proj.T, out_proj.T, jnp.stack([doc_lengths, doc_slot]))

    sums = []
    for b in hop_bits:
        got = swap(send, b)
        size = keep.shape[0] // 2
        total = keep + got
        sums.append(total)
        keep, send = total[:size], total[size:]
    q = jnp.concatenate([queries, got_queries], axis=0)
    q_keep = lax.dynamic_slice_in_dim(q, mine * depth, depth, axis=1)
    q_send = lax.dynamic_slice_in_dim(q, (1 - mine) * depth, depth, axis=1)
    q_bits = (k_bit, top)
    q_parts = (q_keep, swap(q_send, k_bit))
    rest = tuple(b for b in hop_bits[::-1] if b != top)
    for i, b in enumerate(rest):
        q = jnp.concatenate(q_parts, axis=0)
        if i == 0:
            q, _ = lax.optimization_barrier((q, sums[0]))
        q_parts = (q, swap(q, b))
        q_bits = (b,) + q_bits
    got = swap(send, k_bit)

    width = n * per_q
    terms = 8 * per_dev
    left, out = pl.pallas_call(
        functools.partial(near_kernel, per_dev),
        out_shape=(
            jax.ShapeDtypeStruct((terms, depth), BF16),
            jax.ShapeDtypeStruct((width // 2, terms), F32),
        ),
        in_specs=[vmem] * 3,
        out_specs=(vmem, vmem),
        scratch_shapes=[pltpu.VMEM(keep.shape, F32)],
        compiler_params=pltpu.CompilerParams(vmem_limit_bytes=32 << 20),
        cost_estimate=pl.CostEstimate(flops=7000000000, bytes_accessed=1 << 20, transcendentals=0),
        name="near_scores",
    )(keep, got, q_parts[0])
    small = jax.ShapeDtypeStruct((per_dev, width), F32)
    keep, send = pl.pallas_call(
        functools.partial(score_kernel, q_bits, per_dev, per_q),
        out_shape=(small, small),
        in_specs=[vmem] * 3,
        out_specs=(vmem, vmem),
        scratch_shapes=[pltpu.VMEM((width, terms), F32)],
        compiler_params=pltpu.CompilerParams(vmem_limit_bytes=32 << 20),
        name="scores",
    )(left, out, q_parts[1])
    return keep + swap(send, k_bit)


def solution(mesh):
    return jax.shard_map(
        functools.partial(shards, mesh.shape["ctx"]),
        mesh=mesh,
        in_specs=(
            P(("groups", "ctx"), None),
            P(("groups", "ctx"), None),
            P(),
            P(),
            P("groups"),
            P("groups"),
            P("ctx", None),
        ),
        out_specs=P(("groups", "ctx"), None),
        check_vma=False,
    )
```

```python
import functools

import jax
import jax.numpy as jnp
from jax import lax
from jax.experimental import pallas as pl
from jax.experimental.pallas import tpu as pltpu
from jax.sharding import PartitionSpec as P

F32, BF16 = jnp.float32, jnp.bfloat16
LANES = 128
NT = (((1,), (1,)), ((), ()))


def split2(x):
    hi = x.astype(BF16)
    return hi, (x - hi.astype(F32)).astype(BF16)


def low_kernel(
    og_chunk, hid_chunk, hid, og, w_in, w_out, grad_low, input_low,
    hid_v, og_v, w_in_v, w_out_v, og_sem, hid_sem,
):
    tokens = hid.shape[0]
    rank = w_in.shape[0]
    og_pairs, hid_pairs = ((og, og_v), (w_out, w_out_v)), ((hid, hid_v), (w_in, w_in_v))

    def fetches(i, pairs, sems, chunk):
        cols = pl.ds(pl.multiple_of(i * chunk, chunk), chunk)
        return cols, [
            pltpu.make_async_copy(src.at[:, cols], dst.at[:, cols], sems.at[j, i])
            for j, (src, dst) in enumerate(pairs)
        ]

    for i in range(hid.shape[1] // hid_chunk):
        for pairs, sems, chunk in ((og_pairs, og_sem, og_chunk), (hid_pairs, hid_sem, hid_chunk)):
            for copy in fetches(i, pairs, sems, chunk)[1]:
                copy.start()

    def step(i, totals):
        fetched = [
            (pairs, *fetches(i, pairs, sems, chunk))
            for pairs, sems, chunk in ((og_pairs, og_sem, og_chunk), (hid_pairs, hid_sem, hid_chunk))
        ]
        for _, _, copies in fetched:
            for copy in copies:
                copy.wait()
        (_, og_cols, _), (_, hid_cols, _) = fetched
        start, size = hid_cols.start, hid_chunk // 2
        parts = (
            (og_v, w_out_v, og_cols),
            (hid_v, w_in_v, pl.ds(start, size)),
            (hid_v, w_in_v, pl.ds(pl.multiple_of(start + size, size), size)),
        )
        return tuple(
            total + lax.dot_general(x[:, cols], w[:, cols], NT, preferred_element_type=F32)
            for total, (x, w, cols) in zip(totals, parts)
        )

    zeros = jnp.zeros((tokens, rank), F32)
    grad, first, second = lax.fori_loop(0, hid.shape[1] // hid_chunk, step, (zeros,) * 3)
    grad_low[...], input_low[...] = grad.T, (first + second).T


def outer_kernel(
    plan, grad_low, input_low, lengths, slots, keep, send, pair_hi, pair_lo, left
):
    hop_bits, k_bit, per_dev, docs = plan
    rank, tokens = grad_low.shape
    me = lax.axis_index("ctx")

    lane = lax.broadcasted_iota(jnp.int32, (docs, docs), 1)
    sub = lax.broadcasted_iota(jnp.int32, (docs, docs), 0)
    length = jnp.broadcast_to(lengths[...], (docs, docs)).astype(F32)
    slot = jnp.broadcast_to(slots[...], (docs, docs)).astype(F32)
    ends = jnp.sum(jnp.where(lane <= sub, length, 0.0), axis=1, keepdims=True)
    starts = jnp.sum(jnp.where(lane < sub, length, 0.0), axis=1, keepdims=True)
    slot = jnp.sum(jnp.where(lane == sub, slot, 0.0), axis=1, keepdims=True).astype(jnp.int32)
    owner = slot // per_dev
    apart = owner ^ me
    row = jnp.zeros_like(slot)
    for b in hop_bits + (k_bit,):
        row = row * 2 + ((apart >> b) & 1)
    row = (row * per_dev + (slot - owner * per_dev)).astype(F32)
    token = (me * tokens + lax.broadcasted_iota(jnp.int32, (docs, tokens), 1)).astype(F32)
    inside = (token >= starts) & (token < ends)
    token_row = jnp.sum(jnp.where(inside, row, 0.0), axis=0, keepdims=True)

    half = rank // 4
    out_r = lax.broadcasted_iota(jnp.int32, (rank, rank), 0)
    in_r = lax.broadcasted_iota(jnp.int32, (rank, rank), 1)
    odd, p = out_r // (rank // 2), out_r % (rank // 2)
    mine = (me >> k_bit) & 1
    p = (p // half ^ mine) * half + p % half
    order = (in_r == 2 * p + odd).astype(BF16)
    g_hi, g_lo = split2(grad_low[...])
    g_hi = jnp.dot(order, g_hi, preferred_element_type=F32).astype(BF16)
    g_lo = jnp.dot(order, g_lo, preferred_element_type=F32).astype(BF16)
    pairs = rank // 2
    pair_hi[:, :tokens], pair_hi[:, tokens:] = g_hi[:pairs], g_hi[pairs:]
    pair_lo[:, :tokens], pair_lo[:, tokens:] = g_lo[:pairs], g_lo[pairs:]

    x_hi, x_lo = split2(input_low[...])
    zero = jnp.zeros_like(x_hi)

    def diagonal(x):
        return jnp.concatenate(
            [jnp.concatenate([x, zero], axis=1), jnp.concatenate([zero, x], axis=1)], axis=0
        )

    right = jnp.concatenate([diagonal(x_hi), diagonal(x_lo)], axis=0)
    right = jnp.concatenate([right, right], axis=1)

    in_block = 4 * per_dev
    blocks = docs // in_block
    row = 0
    for block in range(blocks):
        for h in range(2):
            rows = pl.ds(h * half, half)
            for s in range(in_block):
                entry = block * in_block + (s ^ (h * per_dev))
                hit = (token_row == float(entry)).astype(F32).astype(BF16)
                hit = jnp.concatenate([hit, hit], axis=1)
                left[row:row + half, :2 * tokens] = pair_hi[rows, :] * hit
                left[row:row + half, 2 * tokens:] = pair_lo[rows, :] * hit
                row += half
    size = keep.shape[0]
    for part, out_ref in enumerate((send, keep)):
        rows = left[(1 - part) * size:(2 - part) * size, :]
        both = lax.dot_general(rows, right, NT, preferred_element_type=F32)
        out_ref[...] = both[:, :LANES] + both[:, LANES:]


def near_kernel(per_dev, grads_a, grads_b, q, left, out, total):
    rows = 2 * per_dev
    tiles = q.shape[1] // LANES
    total[...] = grads_a[...] + grads_b[...]
    pad = jnp.zeros((rows, LANES), BF16)
    for t in range(tiles):
        g = total[pl.ds(t, rows, stride=tiles), :]
        hi = g.astype(BF16)
        mid, low = split2(g - hi.astype(F32))
        left[:, pl.ds(t * LANES, LANES)] = jnp.concatenate([hi, mid, low, pad], axis=0)
    out[...] = lax.dot_general(q[...], left[...], NT, preferred_element_type=F32)


def score_kernel(q_bits, per_dev, per_q, left, out_a, q_b, keep, send, columns):
    me = lax.axis_index("ctx")
    rows = 2 * per_dev
    count = q_b.shape[0]
    out_b = lax.dot_general(q_b[...], left[...], NT, preferred_element_type=F32)
    for part, out in enumerate((out_a[...], out_b)):
        for i in range(count // per_q):
            index = part * (count // per_q) + i
            apart = 0
            for j, b in enumerate(reversed(q_bits)):
                apart = apart | (((index >> j) & 1) << b)
            at = pl.multiple_of((me ^ apart) * per_q, per_q)
            columns[pl.ds(at, per_q), :] = out[i * per_q:(i + 1) * per_q, :]
    out = columns[...].T
    out = out[:rows] + (out[rows:2 * rows] + out[2 * rows:3 * rows])
    keep[...] = out[:per_dev]
    send[...] = out[per_dev:]


def shards(n, hidden, out_grad, in_proj, out_proj, doc_lengths, doc_slot, queries):
    bits = n.bit_length() - 1
    tokens, ff = hidden.shape
    d, rank = out_proj.shape
    docs = doc_slot.shape[0]
    per_dev = docs // n
    per_q = queries.shape[0]
    k_bit, top = 2, bits - 1
    hop_bits = tuple(b for b in range(bits) if b != k_bit)
    me = lax.axis_index("ctx")

    def swap(x, b):
        return lax.ppermute(x, "ctx", [(i, i ^ (1 << b)) for i in range(n)])

    depth = queries.shape[1] // 2
    mine = (me >> k_bit) & 1
    got_queries = swap(queries, top)
    og_chunk, hid_chunk = 1024, 3584
    rows = docs * rank * rank // LANES
    any_spec = pl.BlockSpec(memory_space=pl.ANY)
    vmem = pl.BlockSpec(memory_space=pltpu.VMEM)
    half_shape = jax.ShapeDtypeStruct((rows // 2, LANES), F32)
    low_shape = jax.ShapeDtypeStruct((rank, tokens), F32)
    grad_low, input_low = pl.pallas_call(
        functools.partial(low_kernel, og_chunk, hid_chunk),
        out_shape=(low_shape, low_shape),
        in_specs=[any_spec] * 4,
        out_specs=(vmem, vmem),
        scratch_shapes=[
            pltpu.VMEM((tokens, ff), BF16),
            pltpu.VMEM((tokens, d), BF16),
            pltpu.VMEM((rank, ff), BF16),
            pltpu.VMEM((rank, d), BF16),
            pltpu.SemaphoreType.DMA((2, d // og_chunk)),
            pltpu.SemaphoreType.DMA((2, ff // hid_chunk)),
        ],
        compiler_params=pltpu.CompilerParams(vmem_limit_bytes=(53 << 20) + (1 << 19)),
        cost_estimate=pl.CostEstimate(
            flops=2 * tokens * rank * (ff + d),
            bytes_accessed=2 * (tokens + rank) * (ff + d),
            transcendentals=0,
        ),
        name="low",
    )(hidden, out_grad, in_proj.T, out_proj.T)
    keep, send = pl.pallas_call(
        functools.partial(outer_kernel, (hop_bits, k_bit, per_dev, docs)),
        out_shape=(half_shape, half_shape),
        in_specs=[vmem] * 4,
        out_specs=(vmem, vmem),
        scratch_shapes=[
            pltpu.VMEM((rank // 2, 2 * tokens), BF16),
            pltpu.VMEM((rank // 2, 2 * tokens), BF16),
            pltpu.VMEM((rows, 4 * tokens), BF16),
        ],
        compiler_params=pltpu.CompilerParams(vmem_limit_bytes=32 << 20),
        cost_estimate=pl.CostEstimate(
            flops=2 * rows * 4 * tokens * 2 * LANES, bytes_accessed=1 << 20, transcendentals=0
        ),
        name="outer",
    )(grad_low, input_low, doc_lengths.reshape(1, docs), doc_slot.reshape(1, docs))

    sums = []
    for b in hop_bits[:-1] + (k_bit,):
        got = swap(send, b)
        size = keep.shape[0] // 2
        total = keep + got
        sums.append(total)
        keep, send = total[:size], total[size:]
    q = jnp.concatenate([queries, got_queries], axis=0)
    q_keep = lax.dynamic_slice_in_dim(q, mine * depth, depth, axis=1)
    q_send = lax.dynamic_slice_in_dim(q, (1 - mine) * depth, depth, axis=1)
    q_bits = (k_bit, top)
    q_parts = (q_keep, swap(q_send, k_bit))
    rest = tuple(b for b in hop_bits[::-1] if b != top)
    for i, b in enumerate(rest):
        q = jnp.concatenate(q_parts, axis=0)
        if i == 0:
            q, _ = lax.optimization_barrier((q, sums[0]))
        q_parts = (q, swap(q, b))
        q_bits = (b,) + q_bits
    got = swap(send, top)

    width = n * per_q
    terms = 8 * per_dev
    left, out = pl.pallas_call(
        functools.partial(near_kernel, per_dev),
        out_shape=(
            jax.ShapeDtypeStruct((terms, depth), BF16),
            jax.ShapeDtypeStruct((width // 2, terms), F32),
        ),
        in_specs=[vmem] * 3,
        out_specs=(vmem, vmem),
        scratch_shapes=[pltpu.VMEM(keep.shape, F32)],
        compiler_params=pltpu.CompilerParams(vmem_limit_bytes=32 << 20),
        cost_estimate=pl.CostEstimate(flops=7000000000, bytes_accessed=1 << 20, transcendentals=0),
        name="near_scores",
    )(keep, got, q_parts[0])
    small = jax.ShapeDtypeStruct((per_dev, width), F32)
    keep, send = pl.pallas_call(
        functools.partial(score_kernel, q_bits, per_dev, per_q),
        out_shape=(small, small),
        in_specs=[vmem] * 3,
        out_specs=(vmem, vmem),
        scratch_shapes=[pltpu.VMEM((width, terms), F32)],
        compiler_params=pltpu.CompilerParams(vmem_limit_bytes=32 << 20),
        name="scores",
    )(left, out, q_parts[1])
    return keep + swap(send, k_bit)


def solution(mesh):
    return jax.shard_map(
        functools.partial(shards, mesh.shape["ctx"]),
        mesh=mesh,
        in_specs=(
            P(("groups", "ctx"), None),
            P(("groups", "ctx"), None),
            P(),
            P(),
            P("groups"),
            P("groups"),
            P("ctx", None),
        ),
        out_specs=P(("groups", "ctx"), None),
        check_vma=False,
    )
```

```python
import functools

import jax
import jax.numpy as jnp
from jax import lax
from jax.experimental import pallas as pl
from jax.experimental.pallas import tpu as pltpu
from jax.sharding import PartitionSpec as P

F32, BF16 = jnp.float32, jnp.bfloat16
LANES = 128
NT = (((1,), (1,)), ((), ()))


def split2(x):
    hi = x.astype(BF16)
    return hi, (x - hi.astype(F32)).astype(BF16)


def low_kernel(
    og_chunk, hid_chunk, hid, og, w_in, w_out, grad_low, input_low,
    hid_v, og_v, w_in_v, w_out_v, og_sem, hid_sem,
):
    tokens = hid.shape[0]
    rank = w_in.shape[0]
    og_pairs, hid_pairs = ((og, og_v), (w_out, w_out_v)), ((hid, hid_v), (w_in, w_in_v))

    def fetches(i, pairs, sems, chunk):
        cols = pl.ds(pl.multiple_of(i * chunk, chunk), chunk)
        return cols, [
            pltpu.make_async_copy(src.at[:, cols], dst.at[:, cols], sems.at[j, i])
            for j, (src, dst) in enumerate(pairs)
        ]

    for i in range(hid.shape[1] // hid_chunk):
        for pairs, sems, chunk in ((og_pairs, og_sem, og_chunk), (hid_pairs, hid_sem, hid_chunk)):
            for copy in fetches(i, pairs, sems, chunk)[1]:
                copy.start()

    def step(i, totals):
        fetched = [
            (pairs, *fetches(i, pairs, sems, chunk))
            for pairs, sems, chunk in ((og_pairs, og_sem, og_chunk), (hid_pairs, hid_sem, hid_chunk))
        ]
        for _, _, copies in fetched:
            for copy in copies:
                copy.wait()
        (_, og_cols, _), (_, hid_cols, _) = fetched
        size = hid_chunk // 4
        parts = ((og_v, w_out_v, og_cols),) + tuple(
            (hid_v, w_in_v, pl.ds(pl.multiple_of(hid_cols.start + j * size, LANES), size))
            for j in range(4)
        )
        return tuple(
            total + lax.dot_general(x[:, cols], w[:, cols], NT, preferred_element_type=F32)
            for total, (x, w, cols) in zip(totals, parts)
        )

    zeros = jnp.zeros((tokens, rank), F32)
    grad, *inputs = lax.fori_loop(0, hid.shape[1] // hid_chunk, step, (zeros,) * 5)
    grad_low[...], input_low[...] = grad.T, ((inputs[0] + inputs[1]) + (inputs[2] + inputs[3])).T


def outer_kernel(
    plan, grad_low, input_low, lengths, slots, keep, send, pair_hi, pair_lo, left
):
    hop_bits, k_bit, per_dev, docs = plan
    rank, tokens = grad_low.shape
    me = lax.axis_index("ctx")

    lane = lax.broadcasted_iota(jnp.int32, (docs, docs), 1)
    sub = lax.broadcasted_iota(jnp.int32, (docs, docs), 0)
    length = jnp.broadcast_to(lengths[...], (docs, docs)).astype(F32)
    slot = jnp.broadcast_to(slots[...], (docs, docs)).astype(F32)
    ends = jnp.sum(jnp.where(lane <= sub, length, 0.0), axis=1, keepdims=True)
    starts = jnp.sum(jnp.where(lane < sub, length, 0.0), axis=1, keepdims=True)
    slot = jnp.sum(jnp.where(lane == sub, slot, 0.0), axis=1, keepdims=True).astype(jnp.int32)
    owner = slot // per_dev
    apart = owner ^ me
    row = jnp.zeros_like(slot)
    for b in hop_bits + (k_bit,):
        row = row * 2 + ((apart >> b) & 1)
    row = (row * per_dev + (slot - owner * per_dev)).astype(F32)
    token = (me * tokens + lax.broadcasted_iota(jnp.int32, (docs, tokens), 1)).astype(F32)
    inside = (token >= starts) & (token < ends)
    token_row = jnp.sum(jnp.where(inside, row, 0.0), axis=0, keepdims=True)

    half = rank // 4
    out_r = lax.broadcasted_iota(jnp.int32, (rank, rank), 0)
    in_r = lax.broadcasted_iota(jnp.int32, (rank, rank), 1)
    odd, p = out_r // (rank // 2), out_r % (rank // 2)
    mine = (me >> k_bit) & 1
    p = (p // half ^ mine) * half + p % half
    order = (in_r == 2 * p + odd).astype(BF16)
    g_hi, g_lo = split2(grad_low[...])
    g_hi = jnp.dot(order, g_hi, preferred_element_type=F32).astype(BF16)
    g_lo = jnp.dot(order, g_lo, preferred_element_type=F32).astype(BF16)
    pairs = rank // 2
    pair_hi[:, :tokens], pair_hi[:, tokens:] = g_hi[:pairs], g_hi[pairs:]
    pair_lo[:, :tokens], pair_lo[:, tokens:] = g_lo[:pairs], g_lo[pairs:]

    x_hi, x_lo = split2(input_low[...])
    zero = jnp.zeros_like(x_hi)

    def diagonal(x):
        return jnp.concatenate(
            [jnp.concatenate([x, zero], axis=1), jnp.concatenate([zero, x], axis=1)], axis=0
        )

    right = jnp.concatenate([diagonal(x_hi), diagonal(x_lo)], axis=0)
    right = jnp.concatenate([right, right], axis=1)

    in_block = 4 * per_dev
    blocks = docs // in_block
    row = 0
    for block in range(blocks):
        for h in range(2):
            rows = pl.ds(h * half, half)
            for s in range(in_block):
                entry = block * in_block + (s ^ (h * per_dev))
                hit = (token_row == float(entry)).astype(F32).astype(BF16)
                hit = jnp.concatenate([hit, hit], axis=1)
                left[row:row + half, :2 * tokens] = pair_hi[rows, :] * hit
                left[row:row + half, 2 * tokens:] = pair_lo[rows, :] * hit
                row += half
    size = keep.shape[0]
    for part, out_ref in enumerate((send, keep)):
        rows = left[(1 - part) * size:(2 - part) * size, :]
        both = lax.dot_general(rows, right, NT, preferred_element_type=F32)
        out_ref[...] = both[:, :LANES] + both[:, LANES:]


def near_kernel(per_dev, grads_a, grads_b, q, left, out, total):
    rows = 2 * per_dev
    tiles = q.shape[1] // LANES
    total[...] = grads_a[...] + grads_b[...]
    pad = jnp.zeros((rows, LANES), BF16)
    for t in range(tiles):
        g = total[pl.ds(t, rows, stride=tiles), :]
        hi = g.astype(BF16)
        mid, low = split2(g - hi.astype(F32))
        left[:, pl.ds(t * LANES, LANES)] = jnp.concatenate([hi, mid, low, pad], axis=0)
    out[...] = lax.dot_general(q[...], left[...], NT, preferred_element_type=F32)


def score_kernel(q_bits, per_dev, per_q, left, out_a, q_b, keep, send, columns):
    me = lax.axis_index("ctx")
    rows = 2 * per_dev
    count = q_b.shape[0]
    out_b = lax.dot_general(q_b[...], left[...], NT, preferred_element_type=F32)
    for part, out in enumerate((out_a[...], out_b)):
        for i in range(count // per_q):
            index = part * (count // per_q) + i
            apart = 0
            for j, b in enumerate(reversed(q_bits)):
                apart = apart | (((index >> j) & 1) << b)
            at = pl.multiple_of((me ^ apart) * per_q, per_q)
            columns[pl.ds(at, per_q), :] = out[i * per_q:(i + 1) * per_q, :]
    out = columns[...].T
    out = out[:rows] + (out[rows:2 * rows] + out[2 * rows:3 * rows])
    keep[...] = out[:per_dev]
    send[...] = out[per_dev:]


def shards(n, hidden, out_grad, in_proj, out_proj, doc_lengths, doc_slot, queries):
    bits = n.bit_length() - 1
    tokens, ff = hidden.shape
    d, rank = out_proj.shape
    docs = doc_slot.shape[0]
    per_dev = docs // n
    per_q = queries.shape[0]
    k_bit, top = 1, bits - 1
    hop_bits = tuple(b for b in range(bits) if b != k_bit)
    me = lax.axis_index("ctx")

    def swap(x, b):
        return lax.ppermute(x, "ctx", [(i, i ^ (1 << b)) for i in range(n)])

    depth = queries.shape[1] // 2
    mine = (me >> k_bit) & 1
    got_queries = swap(queries, top)
    og_chunk, hid_chunk = 1024, 3584
    rows = docs * rank * rank // LANES
    any_spec = pl.BlockSpec(memory_space=pl.ANY)
    vmem = pl.BlockSpec(memory_space=pltpu.VMEM)
    half_shape = jax.ShapeDtypeStruct((rows // 2, LANES), F32)
    low_shape = jax.ShapeDtypeStruct((rank, tokens), F32)
    grad_low, input_low = pl.pallas_call(
        functools.partial(low_kernel, og_chunk, hid_chunk),
        out_shape=(low_shape, low_shape),
        in_specs=[any_spec] * 4,
        out_specs=(vmem, vmem),
        scratch_shapes=[
            pltpu.VMEM((tokens, ff), BF16),
            pltpu.VMEM((tokens, d), BF16),
            pltpu.VMEM((rank, ff), BF16),
            pltpu.VMEM((rank, d), BF16),
            pltpu.SemaphoreType.DMA((2, d // og_chunk)),
            pltpu.SemaphoreType.DMA((2, ff // hid_chunk)),
        ],
        compiler_params=pltpu.CompilerParams(vmem_limit_bytes=(53 << 20) + (1 << 19)),
        cost_estimate=pl.CostEstimate(
            flops=2 * tokens * rank * (ff + d),
            bytes_accessed=2 * (tokens + rank) * (ff + d),
            transcendentals=0,
        ),
        name="low",
    )(hidden, out_grad, in_proj.T, out_proj.T)
    keep, send = pl.pallas_call(
        functools.partial(outer_kernel, (hop_bits, k_bit, per_dev, docs)),
        out_shape=(half_shape, half_shape),
        in_specs=[vmem] * 4,
        out_specs=(vmem, vmem),
        scratch_shapes=[
            pltpu.VMEM((rank // 2, 2 * tokens), BF16),
            pltpu.VMEM((rank // 2, 2 * tokens), BF16),
            pltpu.VMEM((rows, 4 * tokens), BF16),
        ],
        compiler_params=pltpu.CompilerParams(vmem_limit_bytes=32 << 20),
        cost_estimate=pl.CostEstimate(
            flops=2 * rows * 4 * tokens * 2 * LANES, bytes_accessed=1 << 20, transcendentals=0
        ),
        name="outer",
    )(grad_low, input_low, doc_lengths.reshape(1, docs), doc_slot.reshape(1, docs))

    sums = []
    for b in hop_bits[:-1] + (k_bit,):
        got = swap(send, b)
        size = keep.shape[0] // 2
        total = keep + got
        sums.append(total)
        keep, send = total[:size], total[size:]
    q = jnp.concatenate([queries, got_queries], axis=0)
    q_keep = lax.dynamic_slice_in_dim(q, mine * depth, depth, axis=1)
    q_send = lax.dynamic_slice_in_dim(q, (1 - mine) * depth, depth, axis=1)
    q_bits = (k_bit, top)
    q_parts = (q_keep, swap(q_send, k_bit))
    rest = tuple(b for b in hop_bits[::-1] if b != top)
    for i, b in enumerate(rest):
        q = jnp.concatenate(q_parts, axis=0)
        if i == 0:
            q, _ = lax.optimization_barrier((q, sums[0]))
        q_parts = (q, swap(q, b))
        q_bits = (b,) + q_bits
    got = swap(send, top)

    width = n * per_q
    terms = 8 * per_dev
    left, out = pl.pallas_call(
        functools.partial(near_kernel, per_dev),
        out_shape=(
            jax.ShapeDtypeStruct((terms, depth), BF16),
            jax.ShapeDtypeStruct((width // 2, terms), F32),
        ),
        in_specs=[vmem] * 3,
        out_specs=(vmem, vmem),
        scratch_shapes=[pltpu.VMEM(keep.shape, F32)],
        compiler_params=pltpu.CompilerParams(vmem_limit_bytes=32 << 20),
        cost_estimate=pl.CostEstimate(flops=7000000000, bytes_accessed=1 << 20, transcendentals=0),
        name="near_scores",
    )(keep, got, q_parts[0])
    small = jax.ShapeDtypeStruct((per_dev, width), F32)
    keep, send = pl.pallas_call(
        functools.partial(score_kernel, q_bits, per_dev, per_q),
        out_shape=(small, small),
        in_specs=[vmem] * 3,
        out_specs=(vmem, vmem),
        scratch_shapes=[pltpu.VMEM((width, terms), F32)],
        compiler_params=pltpu.CompilerParams(vmem_limit_bytes=32 << 20),
        name="scores",
    )(left, out, q_parts[1])
    return keep + swap(send, k_bit)


def solution(mesh):
    return jax.shard_map(
        functools.partial(shards, mesh.shape["ctx"]),
        mesh=mesh,
        in_specs=(
            P(("groups", "ctx"), None),
            P(("groups", "ctx"), None),
            P(),
            P(),
            P("groups"),
            P("groups"),
            P("ctx", None),
        ),
        out_specs=P(("groups", "ctx"), None),
        check_vma=False,
    )
```

```python
import functools

import jax
import jax.numpy as jnp
from jax import lax
from jax.experimental import pallas as pl
from jax.experimental.pallas import tpu as pltpu
from jax.sharding import PartitionSpec as P

F32, BF16 = jnp.float32, jnp.bfloat16
LANES = 128
NT = (((1,), (1,)), ((), ()))


def split2(x):
    hi = x.astype(BF16)
    return hi, (x - hi.astype(F32)).astype(BF16)


def low_kernel(
    og_chunk, hid_chunk, hid, og, w_in, w_out, grad_low, input_low,
    hid_v, og_v, w_in_v, w_out_v, og_sem, hid_sem,
):
    tokens = hid.shape[0]
    rank = w_in.shape[0]
    og_pairs, hid_pairs = ((og, og_v), (w_out, w_out_v)), ((hid, hid_v), (w_in, w_in_v))

    def fetches(i, pairs, sems, chunk):
        cols = pl.ds(pl.multiple_of(i * chunk, chunk), chunk)
        return cols, [
            pltpu.make_async_copy(src.at[:, cols], dst.at[:, cols], sems.at[j, i])
            for j, (src, dst) in enumerate(pairs)
        ]

    for i in range(hid.shape[1] // hid_chunk):
        for pairs, sems, chunk in ((og_pairs, og_sem, og_chunk), (hid_pairs, hid_sem, hid_chunk)):
            for copy in fetches(i, pairs, sems, chunk)[1]:
                copy.start()

    def step(i, totals):
        fetched = [
            (pairs, *fetches(i, pairs, sems, chunk))
            for pairs, sems, chunk in ((og_pairs, og_sem, og_chunk), (hid_pairs, hid_sem, hid_chunk))
        ]
        for _, _, copies in fetched:
            for copy in copies:
                copy.wait()
        (_, og_cols, _), (_, hid_cols, _) = fetched
        start, size = hid_cols.start, hid_chunk // 2
        parts = (
            (og_v, w_out_v, og_cols),
            (hid_v, w_in_v, pl.ds(start, size)),
            (hid_v, w_in_v, pl.ds(pl.multiple_of(start + size, size), size)),
        )
        return tuple(
            total + lax.dot_general(x[:, cols], w[:, cols], NT, preferred_element_type=F32)
            for total, (x, w, cols) in zip(totals, parts)
        )

    zeros = jnp.zeros((tokens, rank), F32)
    grad, first, second = lax.fori_loop(0, hid.shape[1] // hid_chunk, step, (zeros,) * 3)
    grad_low[...], input_low[...] = grad.T, (first + second).T


def outer_kernel(
    plan, part, grad_low, input_low, lengths, slots, out, pair_hi, pair_lo, left
):
    hop_bits, k_bit, per_dev, docs = plan
    rank, tokens = grad_low.shape
    me = lax.axis_index("ctx")

    lane = lax.broadcasted_iota(jnp.int32, (docs, docs), 1)
    sub = lax.broadcasted_iota(jnp.int32, (docs, docs), 0)
    length = jnp.broadcast_to(lengths[...], (docs, docs)).astype(F32)
    slot = jnp.broadcast_to(slots[...], (docs, docs)).astype(F32)
    ends = jnp.sum(jnp.where(lane <= sub, length, 0.0), axis=1, keepdims=True)
    starts = jnp.sum(jnp.where(lane < sub, length, 0.0), axis=1, keepdims=True)
    slot = jnp.sum(jnp.where(lane == sub, slot, 0.0), axis=1, keepdims=True).astype(jnp.int32)
    owner = slot // per_dev
    apart = owner ^ me
    row = jnp.zeros_like(slot)
    for b in hop_bits + (k_bit,):
        row = row * 2 + ((apart >> b) & 1)
    row = (row * per_dev + (slot - owner * per_dev)).astype(F32)
    token = (me * tokens + lax.broadcasted_iota(jnp.int32, (docs, tokens), 1)).astype(F32)
    inside = (token >= starts) & (token < ends)
    token_row = jnp.sum(jnp.where(inside, row, 0.0), axis=0, keepdims=True)

    half = rank // 4
    out_r = lax.broadcasted_iota(jnp.int32, (rank, rank), 0)
    in_r = lax.broadcasted_iota(jnp.int32, (rank, rank), 1)
    odd, p = out_r // (rank // 2), out_r % (rank // 2)
    mine = (me >> k_bit) & 1
    p = (p // half ^ mine) * half + p % half
    order = (in_r == 2 * p + odd).astype(BF16)
    g_hi, g_lo = split2(grad_low[...])
    g_hi = jnp.dot(order, g_hi, preferred_element_type=F32).astype(BF16)
    g_lo = jnp.dot(order, g_lo, preferred_element_type=F32).astype(BF16)
    pairs = rank // 2
    pair_hi[:, :tokens], pair_hi[:, tokens:] = g_hi[:pairs], g_hi[pairs:]
    pair_lo[:, :tokens], pair_lo[:, tokens:] = g_lo[:pairs], g_lo[pairs:]

    x_hi, x_lo = split2(input_low[...])
    zero = jnp.zeros_like(x_hi)

    def diagonal(x):
        return jnp.concatenate(
            [jnp.concatenate([x, zero], axis=1), jnp.concatenate([zero, x], axis=1)], axis=0
        )

    right = jnp.concatenate([diagonal(x_hi), diagonal(x_lo)], axis=0)
    right = jnp.concatenate([right, right], axis=1)

    in_block = 4 * per_dev
    blocks = docs // in_block // 2
    row = 0
    for block in range(part * blocks, (part + 1) * blocks):
        for h in range(2):
            rows = pl.ds(h * half, half)
            for s in range(in_block):
                entry = block * in_block + (s ^ (h * per_dev))
                hit = (token_row == float(entry)).astype(F32).astype(BF16)
                hit = jnp.concatenate([hit, hit], axis=1)
                left[row:row + half, :2 * tokens] = pair_hi[rows, :] * hit
                left[row:row + half, 2 * tokens:] = pair_lo[rows, :] * hit
                row += half
    both = lax.dot_general(left[...], right, NT, preferred_element_type=F32)
    out[...] = both[:, :LANES] + both[:, LANES:]


def near_kernel(per_dev, grads_a, grads_b, q, left, out, total):
    rows = 2 * per_dev
    tiles = q.shape[1] // LANES
    total[...] = grads_a[...] + grads_b[...]
    pad = jnp.zeros((rows, LANES), BF16)
    for t in range(tiles):
        g = total[pl.ds(t, rows, stride=tiles), :]
        hi = g.astype(BF16)
        mid, low = split2(g - hi.astype(F32))
        left[:, pl.ds(t * LANES, LANES)] = jnp.concatenate([hi, mid, low, pad], axis=0)
    out[...] = lax.dot_general(q[...], left[...], NT, preferred_element_type=F32)


def score_kernel(q_bits, per_dev, per_q, left, out_a, q_b, keep, send, columns):
    me = lax.axis_index("ctx")
    rows = 2 * per_dev
    count = q_b.shape[0]
    out_b = lax.dot_general(q_b[...], left[...], NT, preferred_element_type=F32)
    for part, out in enumerate((out_a[...], out_b)):
        for i in range(count // per_q):
            index = part * (count // per_q) + i
            apart = 0
            for j, b in enumerate(reversed(q_bits)):
                apart = apart | (((index >> j) & 1) << b)
            at = pl.multiple_of((me ^ apart) * per_q, per_q)
            columns[pl.ds(at, per_q), :] = out[i * per_q:(i + 1) * per_q, :]
    out = columns[...].T
    out = out[:rows] + (out[rows:2 * rows] + out[2 * rows:3 * rows])
    keep[...] = out[:per_dev]
    send[...] = out[per_dev:]


def shards(n, hidden, out_grad, in_proj, out_proj, doc_lengths, doc_slot, queries):
    bits = n.bit_length() - 1
    tokens, ff = hidden.shape
    d, rank = out_proj.shape
    docs = doc_slot.shape[0]
    per_dev = docs // n
    per_q = queries.shape[0]
    k_bit, top = 2, bits - 1
    hop_bits = tuple(b for b in range(bits) if b != k_bit)
    me = lax.axis_index("ctx")

    def swap(x, b):
        return lax.ppermute(x, "ctx", [(i, i ^ (1 << b)) for i in range(n)])

    depth = queries.shape[1] // 2
    mine = (me >> k_bit) & 1
    got_queries = swap(queries, top)
    og_chunk, hid_chunk = 1024, 3584
    rows = docs * rank * rank // LANES
    any_spec = pl.BlockSpec(memory_space=pl.ANY)
    vmem = pl.BlockSpec(memory_space=pltpu.VMEM)
    half_shape = jax.ShapeDtypeStruct((rows // 2, LANES), F32)
    low_shape = jax.ShapeDtypeStruct((rank, tokens), F32)
    grad_low, input_low = pl.pallas_call(
        functools.partial(low_kernel, og_chunk, hid_chunk),
        out_shape=(low_shape, low_shape),
        in_specs=[any_spec] * 4,
        out_specs=(vmem, vmem),
        scratch_shapes=[
            pltpu.VMEM((tokens, ff), BF16),
            pltpu.VMEM((tokens, d), BF16),
            pltpu.VMEM((rank, ff), BF16),
            pltpu.VMEM((rank, d), BF16),
            pltpu.SemaphoreType.DMA((2, d // og_chunk)),
            pltpu.SemaphoreType.DMA((2, ff // hid_chunk)),
        ],
        compiler_params=pltpu.CompilerParams(vmem_limit_bytes=(53 << 20) + (1 << 19)),
        cost_estimate=pl.CostEstimate(
            flops=2 * tokens * rank * (ff + d),
            bytes_accessed=2 * (tokens + rank) * (ff + d),
            transcendentals=0,
        ),
        name="low",
    )(hidden, out_grad, in_proj.T, out_proj.T)
    keep, send = [
        pl.pallas_call(
            functools.partial(outer_kernel, (hop_bits, k_bit, per_dev, docs), part),
            out_shape=half_shape,
            in_specs=[vmem] * 4,
            out_specs=vmem,
            scratch_shapes=[
                pltpu.VMEM((rank // 2, 2 * tokens), BF16),
                pltpu.VMEM((rank // 2, 2 * tokens), BF16),
                pltpu.VMEM((rows // 2, 4 * tokens), BF16),
            ],
            compiler_params=pltpu.CompilerParams(vmem_limit_bytes=32 << 20),
            cost_estimate=pl.CostEstimate(
                flops=2 * rows * 4 * tokens * LANES, bytes_accessed=1 << 20, transcendentals=0
            ),
            name=name,
        )(grad_low, input_low, doc_lengths.reshape(1, docs), doc_slot.reshape(1, docs))
        for part, name in enumerate(("outer_keep", "outer_send"))
    ]

    sums = []
    for b in hop_bits[:-1] + (k_bit,):
        got = swap(send, b)
        size = keep.shape[0] // 2
        total = keep + got
        sums.append(total)
        keep, send = total[:size], total[size:]
    q = jnp.concatenate([queries, got_queries], axis=0)
    q_keep = lax.dynamic_slice_in_dim(q, mine * depth, depth, axis=1)
    q_send = lax.dynamic_slice_in_dim(q, (1 - mine) * depth, depth, axis=1)
    q_bits = (k_bit, top)
    q_parts = (q_keep, swap(q_send, k_bit))
    rest = tuple(b for b in hop_bits[::-1] if b != top)
    for i, b in enumerate(rest):
        q = jnp.concatenate(q_parts, axis=0)
        if i == 0:
            q, _ = lax.optimization_barrier((q, sums[0]))
        q_parts = (q, swap(q, b))
        q_bits = (b,) + q_bits
    got = swap(send, top)

    width = n * per_q
    terms = 8 * per_dev
    left, out = pl.pallas_call(
        functools.partial(near_kernel, per_dev),
        out_shape=(
            jax.ShapeDtypeStruct((terms, depth), BF16),
            jax.ShapeDtypeStruct((width // 2, terms), F32),
        ),
        in_specs=[vmem] * 3,
        out_specs=(vmem, vmem),
        scratch_shapes=[pltpu.VMEM(keep.shape, F32)],
        compiler_params=pltpu.CompilerParams(vmem_limit_bytes=32 << 20),
        cost_estimate=pl.CostEstimate(flops=7000000000, bytes_accessed=1 << 20, transcendentals=0),
        name="near_scores",
    )(keep, got, q_parts[0])
    small = jax.ShapeDtypeStruct((per_dev, width), F32)
    keep, send = pl.pallas_call(
        functools.partial(score_kernel, q_bits, per_dev, per_q),
        out_shape=(small, small),
        in_specs=[vmem] * 3,
        out_specs=(vmem, vmem),
        scratch_shapes=[pltpu.VMEM((width, terms), F32)],
        compiler_params=pltpu.CompilerParams(vmem_limit_bytes=32 << 20),
        name="scores",
    )(left, out, q_parts[1])
    return keep + swap(send, k_bit)


def solution(mesh):
    return jax.shard_map(
        functools.partial(shards, mesh.shape["ctx"]),
        mesh=mesh,
        in_specs=(
            P(("groups", "ctx"), None),
            P(("groups", "ctx"), None),
            P(),
            P(),
            P("groups"),
            P("groups"),
            P("ctx", None),
        ),
        out_specs=P(("groups", "ctx"), None),
        check_vma=False,
    )
```
